32 devices in a mesh: video: 2 (over x), frame: 4 (over z), head: 4 (over y, core).
Axes of the slice: x: 2, y: 2, z: 4, core: 2. Of those that a mesh axis runs over, the one named last changes fastest.
Arguments:
- latents: bfloat16 [2048, 2560], P(('video', 'frame', 'head')), parts along dimension 0, may hold values from -24 to 24
- weights: bfloat16 [2560, 3, 2560], P(None, None, 'head'), may hold values from -0.125 to 0.125
- key_slots: int32 [16, 4, 4], P('frame'), may hold values from 0 to 3, as said below
- key_count: int32 [16, 4], P('frame'), may hold values from 0 to 4, as said below
Outputs:
- attended: bfloat16 [2048, 2560], P(('video', 'frame'), 'head'), parts along dimension 0
The draws below stay inside these ranges and needn't reach their ends.
There are 2 independent parts, one for each index of `video`. The reference program is written for one: setup_inputs(seed, part) draws one part's arguments, and reference() takes and returns one part's arrays. A program takes and returns all parts, laid end to end along the dimension named above; an argument that names none is the same for every part. Nothing has to cross between parts.
Inputs may be any that keep to these rules, and one draw needn't show every extreme that they name: key_slots[a, b, :] is a permutation of the local block numbers of a slab. key_count[a, b] is 4 when query block a lies in slab b; otherwise it is at most max(1, 4 // p), where p is the largest power of two not above the distance between a's slab and b.
All inputs are finite; a program needn't handle non-finite values.
Results may differ from the reference program's by a relative error of at most 0.012.
The reference program's roundings to bfloat16 on the way count: a program that leaves them out, or rounds other values in their place, can miss the bound.
Values may be sent and summed in bfloat16 or wider, within the bound.
A program may use at most 128 MiB of HBM per device.

```python
import jax
import jax.numpy as jnp
from jax import lax

D = 2560
HEADS = 20
HD = 128
BLK = 64
SLAB = 256
SLABS = 4
SEQ = 1024
BPS = 4
NB = 16


def draw_latents(key, part):
    first = jax.random.fold_in(key, 0)
    base = jax.random.truncated_normal(first, -4.0, 4.0, (SEQ, D), jnp.float32)
    return base.astype(jnp.bfloat16)


def draw_key_slots(key, part):
    ranks = jax.random.randint(key, (NB, SLABS, BPS), 0, 1 << 20, jnp.int32)
    scores = ranks * BPS + jnp.arange(BPS, dtype=jnp.int32)[None, None, :]
    return jnp.argsort(scores, axis=-1).astype(jnp.int32)


def draw_key_count(key, part):
    query_slab = (jnp.arange(NB, dtype=jnp.int32) // BPS)[:, None]
    other_slab = jnp.arange(SLABS, dtype=jnp.int32)[None, :]
    distance = jnp.abs(query_slab - other_slab)
    power = jnp.ones_like(distance)
    for level in range(1, 24):
        power = jnp.where(distance >= 1 << level, 1 << level, power)
    limit = jnp.maximum(BPS // power, 1)
    drawn = jax.random.randint(key, (NB, SLABS), 0, limit + 1, jnp.int32)
    return jnp.where(distance == 0, BPS, drawn).astype(jnp.int32)


def block_scale(key, shape, cuts, smallest, high):
    def one(position, blocks):
        steps = jax.random.uniform(jax.random.fold_in(jax.random.fold_in(key, 6), position), (blocks,), jnp.float32, smallest / len(cuts), high / len(cuts))
        return jnp.repeat(jnp.exp(steps), shape[position] // blocks).reshape((-1,) + (1,) * (len(shape) - position - 1))

    level = one(*cuts[0])
    for cut in cuts[1:]:
        level = level * one(*cut)
    return level


def scatter_about(stream_key, shape, scale, most, cuts=(), kind=jnp.bfloat16):
    array = scale * jax.random.normal(stream_key, shape, jnp.float32)
    if cuts:
        array = array * block_scale(stream_key, shape, cuts, -0.22, 0.18)
    return jnp.clip(array, -most, most).astype(kind)


def setup_inputs(seed: int = 0, part: int = 0) -> dict:
    seeds = jax.random.split(jax.random.key(seed), 5)
    own_keys = jax.random.split(jax.random.fold_in(seeds[4], part), 5)
    return {
        "latents": draw_latents(jax.random.fold_in(jax.random.fold_in(seeds[4], part), 71), part),
        "weights": scatter_about(seeds[1], (D, 3, HEADS * HD), D ** -0.5, 0.125, ((2, 4),)),
        "key_slots": draw_key_slots(jax.random.fold_in(seeds[4], 71), part),
        "key_count": draw_key_count(jax.random.fold_in(seeds[4], 71), part),
    }


def reference(latents, weights, key_slots, key_count):
    width = HEADS * HD
    score_scale = HD ** -0.5
    joined = jnp.dot(latents, weights.reshape(D, 3 * width), preferred_element_type=jnp.float32).astype(jnp.bfloat16)
    queries = joined[:, :width].astype(jnp.float32).reshape(SEQ, HEADS, HD)
    keys_all = joined[:, width:2 * width].astype(jnp.float32).reshape(SEQ, HEADS, HD)
    values_all = joined[:, 2 * width:].astype(jnp.float32).reshape(SEQ, HEADS, HD)
    block_ids = jnp.arange(BPS, dtype=jnp.int32)
    listed = jnp.any((key_slots[:, :, :, None] == block_ids[None, None, None, :]) & (block_ids[None, None, :, None] < key_count[:, :, None, None]), axis=2)
    allowed = listed.reshape(NB, SLABS * BPS)

    def one_slab(slab_index):
        query_part = lax.dynamic_slice_in_dim(queries, slab_index * SLAB, SLAB, 0)
        allow_part = lax.dynamic_slice_in_dim(allowed, slab_index * BPS, BPS, 0)
        visible = jnp.repeat(jnp.repeat(allow_part, BLK, axis=0), BLK, axis=1)
        scores = jnp.einsum("qhd,khd->hqk", query_part, keys_all) * score_scale
        scores = jnp.where(visible[None], scores, -jnp.inf)
        top_score = jnp.max(scores, axis=-1, keepdims=True)
        shares = jnp.exp(scores - top_score)
        share_sum = jnp.sum(shares, axis=-1)
        rounded = lax.optimization_barrier(shares.astype(jnp.bfloat16)).astype(jnp.float32)
        mixed = jnp.einsum("hqk,khd->qhd", rounded, values_all) / jnp.transpose(share_sum)[:, :, None]
        return mixed.reshape(SLAB, width).astype(jnp.bfloat16)

    return lax.map(one_slab, jnp.arange(SLABS, dtype=jnp.int32)).reshape(SEQ, width)
```

```python
import functools

import jax
import jax.numpy as jnp
from jax import lax
from jax.experimental import pallas as pl
from jax.experimental.pallas import tpu as pltpu
from jax.sharding import PartitionSpec as P

HD = 128


masked_score = -1e30
MESH = pl.DeviceIdType.MESH


def on_device(latents, weights, key_slots, key_count):
    width_in = weights.shape[0]
    local_width = weights.shape[2]
    w_joined = weights.reshape(width_in, 3 * local_width)
    joined = jnp.dot(
        lax.all_gather(latents, "head", axis=0, tiled=True),
        w_joined,
        preferred_element_type=jnp.float32,
    ).astype(jnp.bfloat16)
    slab_len = joined.shape[0]
    head_count = local_width // HD
    query_heads = joined[:, :local_width].reshape(slab_len, head_count, HD)
    keys_here = joined[:, local_width : 2 * local_width]
    values_here = joined[:, 2 * local_width :]
    score_scale = HD ** (-0.5)
    blocks_here = key_slots.shape[0]
    slab_total = key_slots.shape[1]
    per_slab = key_slots.shape[2]
    block_rows = slab_len // blocks_here
    all_blocks = slab_total * per_slab
    block_ids = jnp.arange(per_slab, dtype=jnp.int32)
    listed = jnp.any(
        (key_slots[:, :, :, None] == block_ids[None, None, None, :])
        & (block_ids[None, None, :, None] < key_count[:, :, None, None]),
        axis=2,
    )
    allowed = listed.reshape(blocks_here, all_blocks).astype(jnp.float32)

    def compute(state, key_part, value_part, visible):
        row_count = key_part.shape[0]
        top_score, denominator, numerator = state
        scores = (
            jnp.einsum(
                "qhd,khd->hqk",
                query_heads,
                key_part.reshape(row_count, head_count, HD),
                preferred_element_type=jnp.float32,
            )
            * score_scale
        )
        scores = jnp.where(visible[None], scores, masked_score)
        new_top = jnp.maximum(top_score, jnp.max(scores, axis=-1))
        rescale = jnp.exp(top_score - new_top)
        shares = jnp.exp(scores - new_top[:, :, None])
        denominator = denominator * rescale + jnp.sum(shares, axis=-1)
        update = jnp.einsum(
            "hqk,khd->qhd",
            shares.astype(jnp.bfloat16),
            value_part.reshape(row_count, head_count, HD),
            preferred_element_type=jnp.float32,
        )
        numerator = numerator * jnp.transpose(rescale)[:, :, None] + update
        return (new_top, denominator, numerator)

    def attend_rows(running, key_part, value_part, first_row):
        row_count = key_part.shape[0]
        row_blocks = (first_row + jnp.arange(row_count, dtype=jnp.int32)) // block_rows
        onehot = (jnp.arange(all_blocks, dtype=jnp.int32)[:, None] == row_blocks[None, :]).astype(
            jnp.float32
        )
        listed_here = jnp.dot(allowed, onehot) > 0.5
        visible = jnp.broadcast_to(
            listed_here[:, None, :], (blocks_here, block_rows, row_count)
        ).reshape(slab_len, row_count)
        return compute(running, key_part, value_part, visible)

    initial = (
        jnp.full((head_count, slab_len), masked_score, jnp.float32),
        jnp.zeros((head_count, slab_len), jnp.float32),
        jnp.zeros((slab_len, head_count, HD), jnp.float32),
    )
    key_part = lax.all_gather(keys_here, "frame", axis=0, tiled=True)
    value_part = lax.all_gather(values_here, "frame", axis=0, tiled=True)
    row_count = key_part.shape[0]
    step_rows = 512

    def one_block(position, state):
        key_block = lax.dynamic_slice_in_dim(key_part, position * step_rows, step_rows, 0)
        value_block = lax.dynamic_slice_in_dim(value_part, position * step_rows, step_rows, 0)
        return attend_rows(state, key_block, value_block, position * step_rows)

    running = lax.fori_loop(0, row_count // step_rows, one_block, initial)
    top_score, denominator, numerator = running
    mixed = numerator / jnp.transpose(denominator)[:, :, None]
    return mixed.reshape(slab_len, local_width).astype(jnp.bfloat16)


def kernel(lat, w_hbm, slots, count, out, tokens, w, w_sem, kv, q, top, total, acc, send_sem, recv_sem):
    z = lax.axis_index("frame")
    h = lax.axis_index("head")
    core = h % 2
    mate = h + 1 - 2 * core
    across = (h + 2) % 4
    rows, width_in = lat.shape
    width = w_hbm.shape[2]
    slab = 4 * rows
    heads = width // HD
    blocks = slots.shape[0]
    per_slab = slots.shape[2]
    block_rows = slab // blocks
    key_rows = slab // per_slab
    scale = HD ** (-0.5)

    w_copies = [
        pltpu.make_async_copy(w_hbm.at[j], w.at[:, pl.ds(place * width, width)], w_sem.at[place])
        for place, j in enumerate((1, 2, 0))
    ]
    for copy in w_copies:
        copy.start()

    half = z // 2
    end = z + half * (3 - 2 * z)
    firsts = [1 - end, 2, 3]
    others = [f + half * (3 - 2 * f) for f in firsts]

    barrier = pltpu.get_barrier_semaphore()

    def greet(frame, who):
        pl.semaphore_signal(barrier, inc=1, device_id={"frame": frame, "head": who}, device_id_type=MESH)

    greet(z, mate)
    greet(z, across)

    @pl.when(z > 0)
    def _():
        greet(z - 1, h)

    @pl.when(z < 3)
    def _():
        greet(z + 1, h)

    pl.semaphore_wait(barrier, jnp.where(end == 0, 3, 4))

    def copy_of(src, slot, number, frame, who):
        return pltpu.make_async_remote_copy(
            src_ref=src,
            dst_ref=tokens.at[slot],
            send_sem=send_sem.at[number],
            recv_sem=recv_sem.at[slot],
            device_id={"frame": frame, "head": who},
            device_id_type=MESH,
        )

    sends = []

    def send(src, slot, frame, who, when=None):
        copy = copy_of(src, slot, len(sends), frame, who)
        sends.append((copy, when))
        if when is None:
            copy.start()
        else:
            pl.when(when)(copy.start)

    def arrived(slot):
        copy_of(tokens.at[slot], slot, 0, z, mate).wait_recv()

    mine = z * 4 + h
    send(lat, mine, z, across)
    send(lat, mine, z - 1, h, z > 0)
    send(lat, mine, z + 1, h, z < 3)
    send(lat, mine, z, mate)
    tokens[mine] = lat[...]

    def forward(number, when):
        b = others[number]
        slot = b * 4 + h
        sign = jnp.where(b > z, 1, -1)
        onward = z - sign
        goes = (onward >= 0) & (onward <= 3)
        base = 4 + 3 * number
        moves = [
            (copy_of(tokens.at[slot], slot, base, onward, h), goes),
            (copy_of(tokens.at[slot], slot, base + 1, z, across), None),
            (copy_of(tokens.at[slot], slot, base + 2, z, mate), None),
        ]

        def go():
            arrived(slot)
            pl.when(goes)(moves[0][0].start)
            moves[1][0].start()
            moves[2][0].start()

        if when is None:
            go()
        else:
            pl.when(when)(go)
        return moves

    def complete(number, b):
        slot = b * 4 + across
        arrived(slot)
        copy = copy_of(tokens.at[slot], slot, 13 + number, z, mate)
        copy.start()
        arrived(b * 4 + mate)
        arrived(b * 4 + (mate + 2) % 4)
        return [(copy, None)]

    def project(b, first, columns, store):
        x = tokens[pl.ds(b * 4, 4)].reshape(slab, width_in)
        part = jnp.dot(x, w[:, pl.ds(first, columns)], preferred_element_type=jnp.float32)
        store[...] = part.astype(jnp.bfloat16)

    def attend(b, first):
        for tile in range(2 * width // 256):
            project(b, tile * 256, 256, kv.at[:, pl.ds(tile * 256, 256)])
        lane_block = lax.broadcasted_iota(jnp.int32, (1, slab), 1) // key_rows
        shades = []
        for a in range(blocks):
            listed = count[a, b]
            seen = jnp.zeros((1, slab), jnp.float32)
            for s in range(per_slab):
                wanted = jnp.where(s < listed, slots[a, b, s], -1)
                seen = jnp.where(lane_block == wanted, 1.0, seen)
            shade = jnp.where(seen > 0.5, 0.0, masked_score)
            shades.append(jnp.broadcast_to(shade, (block_rows, slab)))
        shade = jnp.concatenate(shades, axis=0)
        for n in range(heads):
            cols = pl.ds(n * HD, HD)
            scores = lax.dot_general(
                q[:, cols], kv[:, cols], (((1,), (1,)), ((), ())), preferred_element_type=jnp.float32
            )
            scores = scores * scale + shade
            peak = jnp.max(scores, axis=1, keepdims=True)
            if not first:
                peak = jnp.maximum(peak, top[n])
            shares = jnp.exp(scores - peak)
            added = jnp.sum(shares, axis=1, keepdims=True)
            mixed = jnp.dot(
                shares.astype(jnp.bfloat16),
                kv[:, pl.ds(width + n * HD, HD)],
                preferred_element_type=jnp.float32,
            )
            if not first:
                keep = jnp.exp(top[n] - peak)
                added = added + total[n] * keep
                mixed = mixed + acc[n] * keep
            top[n] = peak
            total[n] = added
            acc[n] = mixed

    middle = end == 1
    outer = end == 0
    late = []
    late += forward(0, None)
    late += forward(1, middle)
    late += complete(0, z)
    for copy in w_copies:
        copy.wait()
    project(z, 2 * width, width, q)
    attend(z, True)
    forward(1, outer)
    late += forward(2, middle)
    late += complete(1, others[0])
    attend(others[0], False)
    forward(2, outer)
    late += complete(2, others[1])
    attend(others[1], False)
    late += complete(3, others[2])
    attend(others[2], False)
    for n in range(heads):
        out[:, pl.ds(n * HD, HD)] = (acc[n] / total[n]).astype(jnp.bfloat16)
    for copy, when in sends + late:
        if when is None:
            copy.wait_send()
        else:
            pl.when(when)(copy.wait_send)


def fused(latents, weights, key_slots, key_count):
    rows, width_in = latents.shape
    width = weights.shape[2]
    slab = 4 * rows
    heads = width // HD
    return pl.pallas_call(
        kernel,
        out_shape=jax.ShapeDtypeStruct((slab, width), jnp.bfloat16),
        in_specs=[
            pl.BlockSpec(memory_space=pltpu.VMEM),
            pl.BlockSpec(memory_space=pl.ANY),
            pl.BlockSpec(memory_space=pltpu.SMEM),
            pl.BlockSpec(memory_space=pltpu.SMEM),
        ],
        out_specs=pl.BlockSpec(memory_space=pltpu.VMEM),
        scratch_shapes=[
            pltpu.VMEM((16, rows, width_in), jnp.bfloat16),
            pltpu.VMEM((width_in, 3 * width), jnp.bfloat16),
            pltpu.SemaphoreType.DMA((3,)),
            pltpu.VMEM((slab, 2 * width), jnp.bfloat16),
            pltpu.VMEM((slab, width), jnp.bfloat16),
            pltpu.VMEM((heads, slab, 1), jnp.float32),
            pltpu.VMEM((heads, slab, 1), jnp.float32),
            pltpu.VMEM((heads, slab, HD), jnp.float32),
            pltpu.SemaphoreType.DMA((17,)),
            pltpu.SemaphoreType.DMA((16,)),
        ],
        compiler_params=pltpu.CompilerParams(
            collective_id=0, has_side_effects=True, vmem_limit_bytes=48 * 1024 * 1024
        ),
    )(latents, jnp.transpose(weights, (1, 0, 2)), key_slots, key_count)


def solution(mesh):
    small = mesh.shape["frame"] == 4 and mesh.shape["head"] == 4
    return jax.shard_map(
        fused if small else on_device,
        mesh=mesh,
        in_specs=(
            P(("video", "frame", "head"), None),
            P(None, None, "head"),
            P("frame", None, None),
            P("frame", None),
        ),
        out_specs=P(("video", "frame"), "head"),
        check_vma=False,
    )
```

```python
import functools

import jax
import jax.numpy as jnp
from jax import lax
from jax.experimental import pallas as pl
from jax.experimental.pallas import tpu as pltpu
from jax.sharding import PartitionSpec as P

HD = 128


masked_score = -1e30
MESH = pl.DeviceIdType.MESH


def on_device(latents, weights, key_slots, key_count):
    width_in = weights.shape[0]
    local_width = weights.shape[2]
    w_joined = weights.reshape(width_in, 3 * local_width)
    joined = jnp.dot(
        lax.all_gather(latents, "head", axis=0, tiled=True),
        w_joined,
        preferred_element_type=jnp.float32,
    ).astype(jnp.bfloat16)
    slab_len = joined.shape[0]
    head_count = local_width // HD
    query_heads = joined[:, :local_width].reshape(slab_len, head_count, HD)
    keys_here = joined[:, local_width : 2 * local_width]
    values_here = joined[:, 2 * local_width :]
    score_scale = HD ** (-0.5)
    blocks_here = key_slots.shape[0]
    slab_total = key_slots.shape[1]
    per_slab = key_slots.shape[2]
    block_rows = slab_len // blocks_here
    all_blocks = slab_total * per_slab
    block_ids = jnp.arange(per_slab, dtype=jnp.int32)
    listed = jnp.any(
        (key_slots[:, :, :, None] == block_ids[None, None, None, :])
        & (block_ids[None, None, :, None] < key_count[:, :, None, None]),
        axis=2,
    )
    allowed = listed.reshape(blocks_here, all_blocks).astype(jnp.float32)

    def compute(state, key_part, value_part, visible):
        row_count = key_part.shape[0]
        top_score, denominator, numerator = state
        scores = (
            jnp.einsum(
                "qhd,khd->hqk",
                query_heads,
                key_part.reshape(row_count, head_count, HD),
                preferred_element_type=jnp.float32,
            )
            * score_scale
        )
        scores = jnp.where(visible[None], scores, masked_score)
        new_top = jnp.maximum(top_score, jnp.max(scores, axis=-1))
        rescale = jnp.exp(top_score - new_top)
        shares = jnp.exp(scores - new_top[:, :, None])
        denominator = denominator * rescale + jnp.sum(shares, axis=-1)
        update = jnp.einsum(
            "hqk,khd->qhd",
            shares.astype(jnp.bfloat16),
            value_part.reshape(row_count, head_count, HD),
            preferred_element_type=jnp.float32,
        )
        numerator = numerator * jnp.transpose(rescale)[:, :, None] + update
        return (new_top, denominator, numerator)

    def attend_rows(running, key_part, value_part, first_row):
        row_count = key_part.shape[0]
        row_blocks = (first_row + jnp.arange(row_count, dtype=jnp.int32)) // block_rows
        onehot = (jnp.arange(all_blocks, dtype=jnp.int32)[:, None] == row_blocks[None, :]).astype(
            jnp.float32
        )
        listed_here = jnp.dot(allowed, onehot) > 0.5
        visible = jnp.broadcast_to(
            listed_here[:, None, :], (blocks_here, block_rows, row_count)
        ).reshape(slab_len, row_count)
        return compute(running, key_part, value_part, visible)

    initial = (
        jnp.full((head_count, slab_len), masked_score, jnp.float32),
        jnp.zeros((head_count, slab_len), jnp.float32),
        jnp.zeros((slab_len, head_count, HD), jnp.float32),
    )
    key_part = lax.all_gather(keys_here, "frame", axis=0, tiled=True)
    value_part = lax.all_gather(values_here, "frame", axis=0, tiled=True)
    row_count = key_part.shape[0]
    step_rows = 512

    def one_block(position, state):
        key_block = lax.dynamic_slice_in_dim(key_part, position * step_rows, step_rows, 0)
        value_block = lax.dynamic_slice_in_dim(value_part, position * step_rows, step_rows, 0)
        return attend_rows(state, key_block, value_block, position * step_rows)

    running = lax.fori_loop(0, row_count // step_rows, one_block, initial)
    top_score, denominator, numerator = running
    mixed = numerator / jnp.transpose(denominator)[:, :, None]
    return mixed.reshape(slab_len, local_width).astype(jnp.bfloat16)


def kernel(lat, w_hbm, slots_hbm, count_hbm, out, slots, count, local_sem, tokens, w, w_sem, kv, q, top, total, acc, send_sem, recv_sem):
    z = lax.axis_index("frame")
    h = lax.axis_index("head")
    core = h % 2
    mate = h + 1 - 2 * core
    across = (h + 2) % 4
    rows, width_in = lat.shape
    width = w_hbm.shape[2]
    slab = 4 * rows
    heads = width // HD
    blocks = slots.shape[0]
    per_slab = slots.shape[2]
    block_rows = slab // blocks
    key_rows = slab // per_slab
    scale = HD ** (-0.5)

    w_copies = [
        pltpu.make_async_copy(w_hbm.at[j], w.at[:, pl.ds(place * width, width)], w_sem.at[place])
        for place, j in enumerate((1, 2, 0))
    ]
    for copy in w_copies:
        copy.start()

    half = z // 2
    end = z + half * (3 - 2 * z)
    firsts = [1 - end, 2, 3]
    others = [f + half * (3 - 2 * f) for f in firsts]

    barrier = pltpu.get_barrier_semaphore()

    def greet(frame, who):
        pl.semaphore_signal(barrier, inc=1, device_id={"frame": frame, "head": who}, device_id_type=MESH)

    greet(z, mate)
    greet(z, across)

    @pl.when(z > 0)
    def _():
        greet(z - 1, h)

    @pl.when(z < 3)
    def _():
        greet(z + 1, h)

    pl.semaphore_wait(barrier, jnp.where(end == 0, 3, 4))

    def copy_of(src, slot, number, frame, who):
        return pltpu.make_async_remote_copy(
            src_ref=src,
            dst_ref=tokens.at[slot],
            send_sem=send_sem.at[number],
            recv_sem=recv_sem.at[slot],
            device_id={"frame": frame, "head": who},
            device_id_type=MESH,
        )

    sends = []

    def send(src, slot, frame, who, when=None):
        copy = copy_of(src, slot, len(sends), frame, who)
        sends.append((copy, when))
        if when is None:
            copy.start()
        else:
            pl.when(when)(copy.start)

    def arrived(slot):
        copy_of(tokens.at[slot], slot, 0, z, mate).wait_recv()

    mine = z * 4 + h
    send(lat, mine, z, across)
    send(lat, mine, z - 1, h, z > 0)
    send(lat, mine, z + 1, h, z < 3)
    send(lat, mine, z, mate)
    local = [
        pltpu.make_async_copy(lat, tokens.at[mine], local_sem.at[0]),
        pltpu.make_async_copy(slots_hbm, slots, local_sem.at[1]),
        pltpu.make_async_copy(count_hbm, count, local_sem.at[2]),
    ]
    for copy in local:
        copy.start()

    def forward(number, when):
        b = others[number]
        slot = b * 4 + h
        sign = jnp.where(b > z, 1, -1)
        onward = z - sign
        goes = (onward >= 0) & (onward <= 3)
        base = 4 + 3 * number
        moves = [
            (copy_of(tokens.at[slot], slot, base, onward, h), goes),
            (copy_of(tokens.at[slot], slot, base + 1, z, across), None),
            (copy_of(tokens.at[slot], slot, base + 2, z, mate), None),
        ]

        def go():
            arrived(slot)
            pl.when(goes)(moves[0][0].start)
            moves[1][0].start()
            moves[2][0].start()

        if when is None:
            go()
        else:
            pl.when(when)(go)
        return moves

    def complete(number, b):
        slot = b * 4 + across
        arrived(slot)
        copy = copy_of(tokens.at[slot], slot, 13 + number, z, mate)
        copy.start()
        arrived(b * 4 + (mate + 2) % 4)
        return [(copy, None)]

    def project(slot, rows_here, first, columns, store):
        x = tokens[pl.ds(slot, rows_here // rows)].reshape(rows_here, width_in)
        part = jnp.dot(x, w[:, pl.ds(first, columns)], preferred_element_type=jnp.float32)
        store[...] = part.astype(jnp.bfloat16)

    def attend(b, place, length, first):
        span = length * rows
        for tile in range(2 * width // 256):
            project(b * 4 + place, span, tile * 256, 256, kv.at[pl.ds(0, span), pl.ds(tile * 256, 256)])
        lane_block = (lax.broadcasted_iota(jnp.int32, (1, span), 1) + place * rows) // key_rows
        shades = []
        for a in range(blocks):
            listed = count[a, b]
            seen = jnp.zeros((1, span), jnp.float32)
            for s in range(per_slab):
                wanted = jnp.where(s < listed, slots[a, b, s], -1)
                seen = jnp.where(lane_block == wanted, 1.0, seen)
            shade = jnp.where(seen > 0.5, 0.0, masked_score)
            shades.append(jnp.broadcast_to(shade, (block_rows, span)))
        shade = jnp.concatenate(shades, axis=0)
        for n in range(heads):
            cols = pl.ds(n * HD, HD)
            scores = lax.dot_general(
                q[:, cols], kv[pl.ds(0, span), cols], (((1,), (1,)), ((), ())), preferred_element_type=jnp.float32
            )
            scores = scores * scale + shade
            peak = jnp.max(scores, axis=1, keepdims=True)
            if not first:
                peak = jnp.maximum(peak, top[n])
            shares = jnp.exp(scores - peak)
            added = jnp.sum(shares, axis=1, keepdims=True)
            mixed = jnp.dot(
                shares.astype(jnp.bfloat16),
                kv[pl.ds(0, span), pl.ds(width + n * HD, HD)],
                preferred_element_type=jnp.float32,
            )
            if not first:
                keep = jnp.exp(top[n] - peak)
                added = added + total[n] * keep
                mixed = mixed + acc[n] * keep
            top[n] = peak
            total[n] = added
            acc[n] = mixed

    middle = end == 1
    outer = end == 0
    late = []
    late += forward(0, None)
    late += forward(1, middle)
    late += complete(0, z)
    arrived(z * 4 + mate)
    for copy in local + w_copies:
        copy.wait()
    project(z * 4, slab, 2 * width, width, q)
    attend(z, 0, 4, True)
    forward(1, outer)
    late += forward(2, middle)
    late += complete(1, others[0])
    arrived(others[0] * 4 + mate)
    attend(others[0], 0, 4, False)
    forward(2, outer)
    late += complete(2, others[1])
    arrived(others[1] * 4 + mate)
    attend(others[1], 0, 4, False)
    near = 2 * (h // 2)
    arrived(others[2] * 4 + mate)
    attend(others[2], near, 2, False)
    late += complete(3, others[2])
    attend(others[2], 2 - near, 2, False)
    for n in range(heads):
        out[:, pl.ds(n * HD, HD)] = (acc[n] / total[n]).astype(jnp.bfloat16)
    for copy, when in sends + late:
        if when is None:
            copy.wait_send()
        else:
            pl.when(when)(copy.wait_send)


def fused(latents, weights, key_slots, key_count):
    rows, width_in = latents.shape
    width = weights.shape[2]
    slab = 4 * rows
    heads = width // HD
    return pl.pallas_call(
        kernel,
        out_shape=jax.ShapeDtypeStruct((slab, width), jnp.bfloat16),
        in_specs=[
            pl.BlockSpec(memory_space=pltpu.HBM),
            pl.BlockSpec(memory_space=pltpu.HBM),
            pl.BlockSpec(memory_space=pltpu.HBM),
            pl.BlockSpec(memory_space=pltpu.HBM),
        ],
        out_specs=pl.BlockSpec(memory_space=pltpu.VMEM),
        scratch_shapes=[
            pltpu.SMEM(key_slots.shape, jnp.int32),
            pltpu.SMEM(key_count.shape, jnp.int32),
            pltpu.SemaphoreType.DMA((3,)),
            pltpu.VMEM((16, rows, width_in), jnp.bfloat16),
            pltpu.VMEM((width_in, 3 * width), jnp.bfloat16),
            pltpu.SemaphoreType.DMA((3,)),
            pltpu.VMEM((slab, 2 * width), jnp.bfloat16),
            pltpu.VMEM((slab, width), jnp.bfloat16),
            pltpu.VMEM((heads, slab, 1), jnp.float32),
            pltpu.VMEM((heads, slab, 1), jnp.float32),
            pltpu.VMEM((heads, slab, HD), jnp.float32),
            pltpu.SemaphoreType.DMA((17,)),
            pltpu.SemaphoreType.DMA((16,)),
        ],
        compiler_params=pltpu.CompilerParams(
            collective_id=0, has_side_effects=True, vmem_limit_bytes=64 * 1024 * 1024
        ),
    )(latents, jnp.transpose(weights, (1, 0, 2)), key_slots, key_count)


def solution(mesh):
    small = mesh.shape["frame"] == 4 and mesh.shape["head"] == 4
    return jax.shard_map(
        fused if small else on_device,
        mesh=mesh,
        in_specs=(
            P(("video", "frame", "head"), None),
            P(None, None, "head"),
            P("frame", None, None),
            P("frame", None),
        ),
        out_specs=P(("video", "frame"), "head"),
        check_vma=False,
    )
```

```python
import functools

import jax
import jax.numpy as jnp
from jax import lax
from jax.experimental import pallas as pl
from jax.experimental.pallas import tpu as pltpu
from jax.sharding import PartitionSpec as P

HD = 128


masked_score = -1e30
MESH = pl.DeviceIdType.MESH


def on_device(latents, weights, key_slots, key_count):
    width_in = weights.shape[0]
    local_width = weights.shape[2]
    w_joined = weights.reshape(width_in, 3 * local_width)
    joined = jnp.dot(
        lax.all_gather(latents, "head", axis=0, tiled=True),
        w_joined,
        preferred_element_type=jnp.float32,
    ).astype(jnp.bfloat16)
    slab_len = joined.shape[0]
    head_count = local_width // HD
    query_heads = joined[:, :local_width].reshape(slab_len, head_count, HD)
    keys_here = joined[:, local_width : 2 * local_width]
    values_here = joined[:, 2 * local_width :]
    score_scale = HD ** (-0.5)
    blocks_here = key_slots.shape[0]
    slab_total = key_slots.shape[1]
    per_slab = key_slots.shape[2]
    block_rows = slab_len // blocks_here
    all_blocks = slab_total * per_slab
    block_ids = jnp.arange(per_slab, dtype=jnp.int32)
    listed = jnp.any(
        (key_slots[:, :, :, None] == block_ids[None, None, None, :])
        & (block_ids[None, None, :, None] < key_count[:, :, None, None]),
        axis=2,
    )
    allowed = listed.reshape(blocks_here, all_blocks).astype(jnp.float32)

    def compute(state, key_part, value_part, visible):
        row_count = key_part.shape[0]
        top_score, denominator, numerator = state
        scores = (
            jnp.einsum(
                "qhd,khd->hqk",
                query_heads,
                key_part.reshape(row_count, head_count, HD),
                preferred_element_type=jnp.float32,
            )
            * score_scale
        )
        scores = jnp.where(visible[None], scores, masked_score)
        new_top = jnp.maximum(top_score, jnp.max(scores, axis=-1))
        rescale = jnp.exp(top_score - new_top)
        shares = jnp.exp(scores - new_top[:, :, None])
        denominator = denominator * rescale + jnp.sum(shares, axis=-1)
        update = jnp.einsum(
            "hqk,khd->qhd",
            shares.astype(jnp.bfloat16),
            value_part.reshape(row_count, head_count, HD),
            preferred_element_type=jnp.float32,
        )
        numerator = numerator * jnp.transpose(rescale)[:, :, None] + update
        return (new_top, denominator, numerator)

    def attend_rows(running, key_part, value_part, first_row):
        row_count = key_part.shape[0]
        row_blocks = (first_row + jnp.arange(row_count, dtype=jnp.int32)) // block_rows
        onehot = (jnp.arange(all_blocks, dtype=jnp.int32)[:, None] == row_blocks[None, :]).astype(
            jnp.float32
        )
        listed_here = jnp.dot(allowed, onehot) > 0.5
        visible = jnp.broadcast_to(
            listed_here[:, None, :], (blocks_here, block_rows, row_count)
        ).reshape(slab_len, row_count)
        return compute(running, key_part, value_part, visible)

    initial = (
        jnp.full((head_count, slab_len), masked_score, jnp.float32),
        jnp.zeros((head_count, slab_len), jnp.float32),
        jnp.zeros((slab_len, head_count, HD), jnp.float32),
    )
    key_part = lax.all_gather(keys_here, "frame", axis=0, tiled=True)
    value_part = lax.all_gather(values_here, "frame", axis=0, tiled=True)
    row_count = key_part.shape[0]
    step_rows = 512

    def one_block(position, state):
        key_block = lax.dynamic_slice_in_dim(key_part, position * step_rows, step_rows, 0)
        value_block = lax.dynamic_slice_in_dim(value_part, position * step_rows, step_rows, 0)
        return attend_rows(state, key_block, value_block, position * step_rows)

    running = lax.fori_loop(0, row_count // step_rows, one_block, initial)
    top_score, denominator, numerator = running
    mixed = numerator / jnp.transpose(denominator)[:, :, None]
    return mixed.reshape(slab_len, local_width).astype(jnp.bfloat16)


def kernel(lat, w_hbm, slots_hbm, count_hbm, out, slots, count, local_sem, tokens, w, w_sem, kv, q, top, total, acc, send_sem, recv_sem, up_sem):
    z = lax.axis_index("frame")
    h = lax.axis_index("head")
    core = h % 2
    mate = h + 1 - 2 * core
    across = (h + 2) % 4
    rows, width_in = lat.shape
    width = w_hbm.shape[2]
    slab = 4 * rows
    heads = width // HD
    blocks = slots.shape[0]
    per_slab = slots.shape[2]
    block_rows = slab // blocks
    key_rows = slab // per_slab
    scale = HD ** (-0.5)

    w_copies = [
        pltpu.make_async_copy(w_hbm.at[j], w.at[:, pl.ds(place * width, width)], w_sem.at[place])
        for place, j in enumerate((1, 2, 0))
    ]
    for copy in w_copies:
        copy.start()

    half = z // 2
    end = z + half * (3 - 2 * z)
    firsts = [1 - end, 2, 3]
    others = [f + half * (3 - 2 * f) for f in firsts]

    barrier = pltpu.get_barrier_semaphore()

    def greet(frame, who):
        pl.semaphore_signal(barrier, inc=1, device_id={"frame": frame, "head": who}, device_id_type=MESH)

    greet(z, mate)
    greet(z, across)

    @pl.when(z > 0)
    def _():
        greet(z - 1, h)

    @pl.when(z < 3)
    def _():
        greet(z + 1, h)

    pl.semaphore_wait(barrier, jnp.where(end == 0, 3, 4))

    def copy_of(src, slot, number, frame, who):
        return pltpu.make_async_remote_copy(
            src_ref=src,
            dst_ref=tokens.at[slot],
            send_sem=send_sem.at[number],
            recv_sem=recv_sem.at[slot],
            device_id={"frame": frame, "head": who},
            device_id_type=MESH,
        )

    def lower_of(slot, number, frame, who):
        part = tokens.at[slot, pl.ds(0, rows // 2)]
        return pltpu.make_async_remote_copy(
            src_ref=part,
            dst_ref=part,
            send_sem=send_sem.at[number],
            recv_sem=recv_sem.at[slot],
            device_id={"frame": frame, "head": who},
            device_id_type=MESH,
        )

    def upper_of(b, number, frame):
        part = tokens.at[b * 4 + across, pl.ds(rows // 2, rows // 2)]
        return pltpu.make_async_remote_copy(
            src_ref=part,
            dst_ref=tokens.at[b * 4 + across, pl.ds(rows // 2, rows // 2)],
            send_sem=send_sem.at[number],
            recv_sem=up_sem.at[b // 3],
            device_id={"frame": frame, "head": h},
            device_id_type=MESH,
        )

    middle = end == 1
    outer = end == 0
    sends = []

    def send(src, slot, frame, who, when=None):
        copy = copy_of(src, slot, len(sends), frame, who)
        sends.append((copy, when))
        if when is None:
            copy.start()
        else:
            pl.when(when)(copy.start)

    def arrived(slot):
        copy_of(tokens.at[slot], slot, 0, z, mate).wait_recv()

    mine = z * 4 + h
    send(lat, mine, z, across)
    send(lat, mine, z - 1, h, z > 0)
    send(lat, mine, z + 1, h, z < 3)
    send(lat, mine, z, mate)
    local = [
        pltpu.make_async_copy(lat, tokens.at[mine], local_sem.at[0]),
        pltpu.make_async_copy(slots_hbm, slots, local_sem.at[1]),
        pltpu.make_async_copy(count_hbm, count, local_sem.at[2]),
    ]
    for copy in local:
        copy.start()

    def forward(number, when):
        b = others[number]
        slot = b * 4 + h
        sign = jnp.where(b > z, 1, -1)
        onward = z - sign
        goes = (onward >= 0) & (onward <= 3)
        base = 4 + 3 * number
        moves = [
            (copy_of(tokens.at[slot], slot, base, onward, h), goes),
            (copy_of(tokens.at[slot], slot, base + 2, z, mate), None),
        ]
        if number == 0:
            moves.append((copy_of(tokens.at[slot], slot, base + 1, z, across), outer))
            moves.append((lower_of(slot, base + 1, z, across), middle))
        elif number == 1:
            moves.append((copy_of(tokens.at[slot], slot, base + 1, z, across), None))
        else:
            moves.append((lower_of(slot, base + 1, z, across), None))

        def go():
            arrived(slot)
            for copy, wanted in moves[:1] + moves[2:] + moves[1:2]:
                if wanted is None:
                    copy.start()
                else:
                    pl.when(wanted)(copy.start)

        if when is None:
            go()
        else:
            pl.when(when)(go)
        return moves

    def complete(number, b):
        slot = b * 4 + across
        if number == 1:

            @pl.when(outer)
            def _():
                arrived(slot)

            @pl.when(middle)
            def _():
                lower_of(slot, 0, z, mate).wait_recv()

        elif number == 3:
            lower_of(slot, 0, z, mate).wait_recv()

            @pl.when(outer)
            def _():
                upper_of(b, 0, z + 1 - 2 * half).wait_recv()

        else:
            arrived(slot)
        copy = copy_of(tokens.at[slot], slot, 13 + number, z, mate)
        copy.start()
        arrived(b * 4 + (mate + 2) % 4)
        return [(copy, None)]

    inward = z + 1 - 2 * half

    def pass_upper(b, number, frame):
        copy = upper_of(b, number, frame)

        @pl.when(middle)
        def _():
            copy.wait_recv()
            copy.start()

        return [(copy, middle)]

    def project(slot, rows_here, first, columns, store):
        x = tokens[pl.ds(slot, rows_here // rows)].reshape(rows_here, width_in)
        part = jnp.dot(x, w[:, pl.ds(first, columns)], preferred_element_type=jnp.float32)
        store[...] = part.astype(jnp.bfloat16)

    def attend(b, place, length, first):
        span = length * rows
        for tile in range(2 * width // 256):
            project(b * 4 + place, span, tile * 256, 256, kv.at[pl.ds(0, span), pl.ds(tile * 256, 256)])
        lane_block = (lax.broadcasted_iota(jnp.int32, (1, span), 1) + place * rows) // key_rows
        shades = []
        for a in range(blocks):
            listed = count[a, b]
            seen = jnp.zeros((1, span), jnp.float32)
            for s in range(per_slab):
                wanted = jnp.where(s < listed, slots[a, b, s], -1)
                seen = jnp.where(lane_block == wanted, 1.0, seen)
            shade = jnp.where(seen > 0.5, 0.0, masked_score)
            shades.append(jnp.broadcast_to(shade, (block_rows, span)))
        shade = jnp.concatenate(shades, axis=0)
        for n in range(heads):
            cols = pl.ds(n * HD, HD)
            scores = lax.dot_general(
                q[:, cols], kv[pl.ds(0, span), cols], (((1,), (1,)), ((), ())), preferred_element_type=jnp.float32
            )
            scores = scores * scale + shade
            peak = jnp.max(scores, axis=1, keepdims=True)
            if not first:
                peak = jnp.maximum(peak, top[n])
            shares = jnp.exp(scores - peak)
            added = jnp.sum(shares, axis=1, keepdims=True)
            mixed = jnp.dot(
                shares.astype(jnp.bfloat16),
                kv[pl.ds(0, span), pl.ds(width + n * HD, HD)],
                preferred_element_type=jnp.float32,
            )
            if not first:
                keep = jnp.exp(top[n] - peak)
                added = added + total[n] * keep
                mixed = mixed + acc[n] * keep
            top[n] = peak
            total[n] = added
            acc[n] = mixed

    late = []
    late += forward(0, None)
    late += forward(1, middle)
    late += complete(0, z)
    own_upper = upper_of(z, 17, inward)
    pl.when(outer)(own_upper.start)
    late.append((own_upper, outer))
    arrived(z * 4 + mate)
    for copy in local + w_copies:
        copy.wait()
    project(z * 4, slab, 2 * width, width, q)
    attend(z, 0, 4, True)
    forward(1, outer)
    late += forward(2, middle)
    late += pass_upper(others[0], 18, inward)
    late += complete(1, others[0])
    arrived(others[0] * 4 + mate)
    attend(others[0], 0, 4, False)
    forward(2, outer)
    late += pass_upper(others[2], 19, z - 1 + 2 * half)
    late += complete(2, others[1])
    arrived(others[1] * 4 + mate)
    attend(others[1], 0, 4, False)
    near = 2 * (h // 2)
    arrived(others[2] * 4 + mate)
    attend(others[2], near, 2, False)
    late += complete(3, others[2])
    attend(others[2], 2 - near, 2, False)
    for n in range(heads):
        out[:, pl.ds(n * HD, HD)] = (acc[n] / total[n]).astype(jnp.bfloat16)
    for copy, when in sends + late:
        if when is None:
            copy.wait_send()
        else:
            pl.when(when)(copy.wait_send)


def fused(latents, weights, key_slots, key_count):
    rows, width_in = latents.shape
    width = weights.shape[2]
    slab = 4 * rows
    heads = width // HD
    return pl.pallas_call(
        kernel,
        out_shape=jax.ShapeDtypeStruct((slab, width), jnp.bfloat16),
        in_specs=[
            pl.BlockSpec(memory_space=pltpu.HBM),
            pl.BlockSpec(memory_space=pltpu.HBM),
            pl.BlockSpec(memory_space=pltpu.HBM),
            pl.BlockSpec(memory_space=pltpu.HBM),
        ],
        out_specs=pl.BlockSpec(memory_space=pltpu.VMEM),
        scratch_shapes=[
            pltpu.SMEM(key_slots.shape, jnp.int32),
            pltpu.SMEM(key_count.shape, jnp.int32),
            pltpu.SemaphoreType.DMA((3,)),
            pltpu.VMEM((16, rows, width_in), jnp.bfloat16),
            pltpu.VMEM((width_in, 3 * width), jnp.bfloat16),
            pltpu.SemaphoreType.DMA((3,)),
            pltpu.VMEM((slab, 2 * width), jnp.bfloat16),
            pltpu.VMEM((slab, width), jnp.bfloat16),
            pltpu.VMEM((heads, slab, 1), jnp.float32),
            pltpu.VMEM((heads, slab, 1), jnp.float32),
            pltpu.VMEM((heads, slab, HD), jnp.float32),
            pltpu.SemaphoreType.DMA((20,)),
            pltpu.SemaphoreType.DMA((16,)),
            pltpu.SemaphoreType.DMA((2,)),
        ],
        compiler_params=pltpu.CompilerParams(
            collective_id=0, has_side_effects=True, vmem_limit_bytes=64 * 1024 * 1024
        ),
    )(latents, jnp.transpose(weights, (1, 0, 2)), key_slots, key_count)


def solution(mesh):
    small = mesh.shape["frame"] == 4 and mesh.shape["head"] == 4
    return jax.shard_map(
        fused if small else on_device,
        mesh=mesh,
        in_specs=(
            P(("video", "frame", "head"), None),
            P(None, None, "head"),
            P("frame", None, None),
            P("frame", None),
        ),
        out_specs=P(("video", "frame"), "head"),
        check_vma=False,
    )
```

```python
import functools

import jax
import jax.numpy as jnp
from jax import lax
from jax.experimental import pallas as pl
from jax.experimental.pallas import tpu as pltpu
from jax.sharding import PartitionSpec as P

HD = 128


masked_score = -1e30
MESH = pl.DeviceIdType.MESH


def on_device(latents, weights, key_slots, key_count):
    width_in = weights.shape[0]
    local_width = weights.shape[2]
    w_joined = weights.reshape(width_in, 3 * local_width)
    joined = jnp.dot(
        lax.all_gather(latents, "head", axis=0, tiled=True),
        w_joined,
        preferred_element_type=jnp.float32,
    ).astype(jnp.bfloat16)
    slab_len = joined.shape[0]
    head_count = local_width // HD
    query_heads = joined[:, :local_width].reshape(slab_len, head_count, HD)
    keys_here = joined[:, local_width : 2 * local_width]
    values_here = joined[:, 2 * local_width :]
    score_scale = HD ** (-0.5)
    blocks_here = key_slots.shape[0]
    slab_total = key_slots.shape[1]
    per_slab = key_slots.shape[2]
    block_rows = slab_len // blocks_here
    all_blocks = slab_total * per_slab
    block_ids = jnp.arange(per_slab, dtype=jnp.int32)
    listed = jnp.any(
        (key_slots[:, :, :, None] == block_ids[None, None, None, :])
        & (block_ids[None, None, :, None] < key_count[:, :, None, None]),
        axis=2,
    )
    allowed = listed.reshape(blocks_here, all_blocks).astype(jnp.float32)

    def compute(state, key_part, value_part, visible):
        row_count = key_part.shape[0]
        top_score, denominator, numerator = state
        scores = (
            jnp.einsum(
                "qhd,khd->hqk",
                query_heads,
                key_part.reshape(row_count, head_count, HD),
                preferred_element_type=jnp.float32,
            )
            * score_scale
        )
        scores = jnp.where(visible[None], scores, masked_score)
        new_top = jnp.maximum(top_score, jnp.max(scores, axis=-1))
        rescale = jnp.exp(top_score - new_top)
        shares = jnp.exp(scores - new_top[:, :, None])
        denominator = denominator * rescale + jnp.sum(shares, axis=-1)
        update = jnp.einsum(
            "hqk,khd->qhd",
            shares.astype(jnp.bfloat16),
            value_part.reshape(row_count, head_count, HD),
            preferred_element_type=jnp.float32,
        )
        numerator = numerator * jnp.transpose(rescale)[:, :, None] + update
        return (new_top, denominator, numerator)

    def attend_rows(running, key_part, value_part, first_row):
        row_count = key_part.shape[0]
        row_blocks = (first_row + jnp.arange(row_count, dtype=jnp.int32)) // block_rows
        onehot = (jnp.arange(all_blocks, dtype=jnp.int32)[:, None] == row_blocks[None, :]).astype(
            jnp.float32
        )
        listed_here = jnp.dot(allowed, onehot) > 0.5
        visible = jnp.broadcast_to(
            listed_here[:, None, :], (blocks_here, block_rows, row_count)
        ).reshape(slab_len, row_count)
        return compute(running, key_part, value_part, visible)

    initial = (
        jnp.full((head_count, slab_len), masked_score, jnp.float32),
        jnp.zeros((head_count, slab_len), jnp.float32),
        jnp.zeros((slab_len, head_count, HD), jnp.float32),
    )
    key_part = lax.all_gather(keys_here, "frame", axis=0, tiled=True)
    value_part = lax.all_gather(values_here, "frame", axis=0, tiled=True)
    row_count = key_part.shape[0]
    step_rows = 512

    def one_block(position, state):
        key_block = lax.dynamic_slice_in_dim(key_part, position * step_rows, step_rows, 0)
        value_block = lax.dynamic_slice_in_dim(value_part, position * step_rows, step_rows, 0)
        return attend_rows(state, key_block, value_block, position * step_rows)

    running = lax.fori_loop(0, row_count // step_rows, one_block, initial)
    top_score, denominator, numerator = running
    mixed = numerator / jnp.transpose(denominator)[:, :, None]
    return mixed.reshape(slab_len, local_width).astype(jnp.bfloat16)


def kernel(lat, w_hbm, slots_hbm, count_hbm, out, slots, count, local_sem, tokens, w, w_sem, kv, q, top, total, acc, send_sem, recv_sem, up_sem):
    z = lax.axis_index("frame")
    h = lax.axis_index("head")
    core = h % 2
    mate = h + 1 - 2 * core
    across = (h + 2) % 4
    rows, width_in = lat.shape
    width = w_hbm.shape[2]
    slab = 4 * rows
    heads = width // HD
    blocks = slots.shape[0]
    per_slab = slots.shape[2]
    block_rows = slab // blocks
    key_rows = slab // per_slab
    scale = HD ** (-0.5) * 1.4426950408889634

    w_copies = [
        pltpu.make_async_copy(w_hbm.at[j], w.at[:, pl.ds(place * width, width)], w_sem.at[place])
        for place, j in enumerate((1, 2, 0))
    ]
    for copy in w_copies:
        copy.start()

    half = z // 2
    end = z + half * (3 - 2 * z)
    firsts = [1 - end, 2, 3]
    others = [f + half * (3 - 2 * f) for f in firsts]

    barrier = pltpu.get_barrier_semaphore()

    def greet(frame, who):
        pl.semaphore_signal(barrier, inc=1, device_id={"frame": frame, "head": who}, device_id_type=MESH)

    greet(z, mate)
    greet(z, across)

    @pl.when(z > 0)
    def _():
        greet(z - 1, h)

    @pl.when(z < 3)
    def _():
        greet(z + 1, h)

    pl.semaphore_wait(barrier, jnp.where(end == 0, 3, 4))

    def copy_of(src, slot, number, frame, who):
        return pltpu.make_async_remote_copy(
            src_ref=src,
            dst_ref=tokens.at[slot],
            send_sem=send_sem.at[number],
            recv_sem=recv_sem.at[slot],
            device_id={"frame": frame, "head": who},
            device_id_type=MESH,
        )

    def lower_of(slot, number, frame, who):
        part = tokens.at[slot, pl.ds(0, rows // 2)]
        return pltpu.make_async_remote_copy(
            src_ref=part,
            dst_ref=part,
            send_sem=send_sem.at[number],
            recv_sem=recv_sem.at[slot],
            device_id={"frame": frame, "head": who},
            device_id_type=MESH,
        )

    def upper_of(b, number, frame):
        part = tokens.at[b * 4 + across, pl.ds(rows // 2, rows // 2)]
        return pltpu.make_async_remote_copy(
            src_ref=part,
            dst_ref=tokens.at[b * 4 + across, pl.ds(rows // 2, rows // 2)],
            send_sem=send_sem.at[number],
            recv_sem=up_sem.at[b // 3],
            device_id={"frame": frame, "head": h},
            device_id_type=MESH,
        )

    middle = end == 1
    outer = end == 0
    sends = []

    def send(src, slot, frame, who, when=None):
        copy = copy_of(src, slot, len(sends), frame, who)
        sends.append((copy, when))
        if when is None:
            copy.start()
        else:
            pl.when(when)(copy.start)

    def arrived(slot):
        copy_of(tokens.at[slot], slot, 0, z, mate).wait_recv()

    mine = z * 4 + h
    send(lat, mine, z, across)
    send(lat, mine, z - 1, h, z > 0)
    send(lat, mine, z + 1, h, z < 3)
    send(lat, mine, z, mate)
    local = [
        pltpu.make_async_copy(lat, tokens.at[mine], local_sem.at[0]),
        pltpu.make_async_copy(slots_hbm, slots, local_sem.at[1]),
        pltpu.make_async_copy(count_hbm, count, local_sem.at[2]),
    ]
    for copy in local:
        copy.start()

    def forward(number, when):
        b = others[number]
        slot = b * 4 + h
        sign = jnp.where(b > z, 1, -1)
        onward = z - sign
        goes = (onward >= 0) & (onward <= 3)
        base = 4 + 3 * number
        moves = [
            (copy_of(tokens.at[slot], slot, base, onward, h), goes),
            (copy_of(tokens.at[slot], slot, base + 2, z, mate), None),
        ]
        if number == 0:
            moves.append((copy_of(tokens.at[slot], slot, base + 1, z, across), outer))
            moves.append((lower_of(slot, base + 1, z, across), middle))
        elif number == 1:
            moves.append((copy_of(tokens.at[slot], slot, base + 1, z, across), None))
        else:
            moves.append((lower_of(slot, base + 1, z, across), None))

        def go():
            arrived(slot)
            for copy, wanted in moves[:1] + moves[2:] + moves[1:2]:
                if wanted is None:
                    copy.start()
                else:
                    pl.when(wanted)(copy.start)

        if when is None:
            go()
        else:
            pl.when(when)(go)
        return moves

    def complete(number, b):
        slot = b * 4 + across
        if number == 1:

            @pl.when(outer)
            def _():
                arrived(slot)

            @pl.when(middle)
            def _():
                lower_of(slot, 0, z, mate).wait_recv()

        elif number == 3:
            lower_of(slot, 0, z, mate).wait_recv()

            @pl.when(outer)
            def _():
                upper_of(b, 0, z + 1 - 2 * half).wait_recv()

        else:
            arrived(slot)
        copy = copy_of(tokens.at[slot], slot, 13 + number, z, mate)
        copy.start()
        arrived(b * 4 + (mate + 2) % 4)
        return [(copy, None)]

    inward = z + 1 - 2 * half

    def pass_upper(b, number, frame):
        copy = upper_of(b, number, frame)

        @pl.when(middle)
        def _():
            copy.wait_recv()
            copy.start()

        return [(copy, middle)]

    def project(slot, rows_here, first, columns, store):
        x = tokens[pl.ds(slot, rows_here // rows)].reshape(rows_here, width_in)
        part = jnp.dot(x, w[:, pl.ds(first, columns)], preferred_element_type=jnp.float32)
        store[...] = part.astype(jnp.bfloat16)

    def attend(b, place, length, first):
        span = length * rows
        for tile in range(2 * width // 256):
            project(b * 4 + place, span, tile * 256, 256, kv.at[pl.ds(0, span), pl.ds(tile * 256, 256)])
        lane_block = (lax.broadcasted_iota(jnp.int32, (1, span), 1) + place * rows) // key_rows
        shades = []
        for a in range(blocks):
            listed = count[a, b]
            seen = jnp.zeros((1, span), jnp.float32)
            for s in range(per_slab):
                wanted = jnp.where(s < listed, slots[a, b, s], -1)
                seen = jnp.where(lane_block == wanted, 1.0, seen)
            shade = jnp.where(seen > 0.5, 0.0, masked_score)
            shades.append(jnp.broadcast_to(shade, (block_rows, span)))
        shade = jnp.concatenate(shades, axis=0)
        for n in range(heads):
            cols = pl.ds(n * HD, HD)
            scores = lax.dot_general(
                q[:, cols], kv[pl.ds(0, span), cols], (((1,), (1,)), ((), ())), preferred_element_type=jnp.float32
            )
            scores = scores * scale + shade
            peak = jnp.max(scores, axis=1, keepdims=True)
            if not first:
                peak = jnp.maximum(peak, top[n])
            shares = jnp.exp2(scores - peak)
            added = jnp.sum(shares, axis=1, keepdims=True)
            mixed = jnp.dot(
                shares.astype(jnp.bfloat16),
                kv[pl.ds(0, span), pl.ds(width + n * HD, HD)],
                preferred_element_type=jnp.float32,
            )
            if not first:
                keep = jnp.exp2(top[n] - peak)
                added = added + total[n] * keep
                mixed = mixed + acc[n] * keep
            top[n] = peak
            total[n] = added
            acc[n] = mixed

    late = []
    late += forward(0, None)
    late += forward(1, middle)
    late += complete(0, z)
    own_upper = upper_of(z, 17, inward)
    pl.when(outer)(own_upper.start)
    late.append((own_upper, outer))
    arrived(z * 4 + mate)
    for copy in local + w_copies:
        copy.wait()
    project(z * 4, slab, 2 * width, width, q)
    attend(z, 0, 4, True)
    forward(1, outer)
    late += forward(2, middle)
    late += pass_upper(others[0], 18, inward)
    late += complete(1, others[0])
    arrived(others[0] * 4 + mate)
    attend(others[0], 0, 4, False)
    forward(2, outer)
    late += pass_upper(others[2], 19, z - 1 + 2 * half)
    late += complete(2, others[1])
    arrived(others[1] * 4 + mate)
    attend(others[1], 0, 4, False)
    arrived(others[2] * 4 + mate)
    late += complete(3, others[2])
    attend(others[2], 0, 4, False)
    for n in range(heads):
        out[:, pl.ds(n * HD, HD)] = (acc[n] / total[n]).astype(jnp.bfloat16)
    for copy, when in sends + late:
        if when is None:
            copy.wait_send()
        else:
            pl.when(when)(copy.wait_send)


def fused(latents, weights, key_slots, key_count):
    rows, width_in = latents.shape
    width = weights.shape[2]
    slab = 4 * rows
    heads = width // HD
    return pl.pallas_call(
        kernel,
        out_shape=jax.ShapeDtypeStruct((slab, width), jnp.bfloat16),
        in_specs=[
            pl.BlockSpec(memory_space=pltpu.HBM),
            pl.BlockSpec(memory_space=pltpu.HBM),
            pl.BlockSpec(memory_space=pltpu.HBM),
            pl.BlockSpec(memory_space=pltpu.HBM),
        ],
        out_specs=pl.BlockSpec(memory_space=pltpu.VMEM),
        scratch_shapes=[
            pltpu.SMEM(key_slots.shape, jnp.int32),
            pltpu.SMEM(key_count.shape, jnp.int32),
            pltpu.SemaphoreType.DMA((3,)),
            pltpu.VMEM((16, rows, width_in), jnp.bfloat16),
            pltpu.VMEM((width_in, 3 * width), jnp.bfloat16),
            pltpu.SemaphoreType.DMA((3,)),
            pltpu.VMEM((slab, 2 * width), jnp.bfloat16),
            pltpu.VMEM((slab, width), jnp.bfloat16),
            pltpu.VMEM((heads, slab, 1), jnp.float32),
            pltpu.VMEM((heads, slab, 1), jnp.float32),
            pltpu.VMEM((heads, slab, HD), jnp.float32),
            pltpu.SemaphoreType.DMA((20,)),
            pltpu.SemaphoreType.DMA((16,)),
            pltpu.SemaphoreType.DMA((2,)),
        ],
        compiler_params=pltpu.CompilerParams(
            collective_id=0, has_side_effects=True, vmem_limit_bytes=64 * 1024 * 1024
        ),
    )(latents, jnp.transpose(weights, (1, 0, 2)), key_slots, key_count)


def solution(mesh):
    small = mesh.shape["frame"] == 4 and mesh.shape["head"] == 4
    return jax.shard_map(
        fused if small else on_device,
        mesh=mesh,
        in_specs=(
            P(("video", "frame", "head"), None),
            P(None, None, "head"),
            P("frame", None, None),
            P("frame", None),
        ),
        out_specs=P(("video", "frame"), "head"),
        check_vma=False,
    )
```

```python
import functools

import jax
import jax.numpy as jnp
from jax import lax
from jax.experimental import pallas as pl
from jax.experimental.pallas import tpu as pltpu
from jax.sharding import PartitionSpec as P

HD = 128


masked_score = -1e30
MESH = pl.DeviceIdType.MESH


def on_device(latents, weights, key_slots, key_count):
    width_in = weights.shape[0]
    local_width = weights.shape[2]
    w_joined = weights.reshape(width_in, 3 * local_width)
    joined = jnp.dot(
        lax.all_gather(latents, "head", axis=0, tiled=True),
        w_joined,
        preferred_element_type=jnp.float32,
    ).astype(jnp.bfloat16)
    slab_len = joined.shape[0]
    head_count = local_width // HD
    query_heads = joined[:, :local_width].reshape(slab_len, head_count, HD)
    keys_here = joined[:, local_width : 2 * local_width]
    values_here = joined[:, 2 * local_width :]
    score_scale = HD ** (-0.5)
    blocks_here = key_slots.shape[0]
    slab_total = key_slots.shape[1]
    per_slab = key_slots.shape[2]
    block_rows = slab_len // blocks_here
    all_blocks = slab_total * per_slab
    block_ids = jnp.arange(per_slab, dtype=jnp.int32)
    listed = jnp.any(
        (key_slots[:, :, :, None] == block_ids[None, None, None, :])
        & (block_ids[None, None, :, None] < key_count[:, :, None, None]),
        axis=2,
    )
    allowed = listed.reshape(blocks_here, all_blocks).astype(jnp.float32)

    def compute(state, key_part, value_part, visible):
        row_count = key_part.shape[0]
        top_score, denominator, numerator = state
        scores = (
            jnp.einsum(
                "qhd,khd->hqk",
                query_heads,
                key_part.reshape(row_count, head_count, HD),
                preferred_element_type=jnp.float32,
            )
            * score_scale
        )
        scores = jnp.where(visible[None], scores, masked_score)
        new_top = jnp.maximum(top_score, jnp.max(scores, axis=-1))
        rescale = jnp.exp(top_score - new_top)
        shares = jnp.exp(scores - new_top[:, :, None])
        denominator = denominator * rescale + jnp.sum(shares, axis=-1)
        update = jnp.einsum(
            "hqk,khd->qhd",
            shares.astype(jnp.bfloat16),
            value_part.reshape(row_count, head_count, HD),
            preferred_element_type=jnp.float32,
        )
        numerator = numerator * jnp.transpose(rescale)[:, :, None] + update
        return (new_top, denominator, numerator)

    def attend_rows(running, key_part, value_part, first_row):
        row_count = key_part.shape[0]
        row_blocks = (first_row + jnp.arange(row_count, dtype=jnp.int32)) // block_rows
        onehot = (jnp.arange(all_blocks, dtype=jnp.int32)[:, None] == row_blocks[None, :]).astype(
            jnp.float32
        )
        listed_here = jnp.dot(allowed, onehot) > 0.5
        visible = jnp.broadcast_to(
            listed_here[:, None, :], (blocks_here, block_rows, row_count)
        ).reshape(slab_len, row_count)
        return compute(running, key_part, value_part, visible)

    initial = (
        jnp.full((head_count, slab_len), masked_score, jnp.float32),
        jnp.zeros((head_count, slab_len), jnp.float32),
        jnp.zeros((slab_len, head_count, HD), jnp.float32),
    )
    key_part = lax.all_gather(keys_here, "frame", axis=0, tiled=True)
    value_part = lax.all_gather(values_here, "frame", axis=0, tiled=True)
    row_count = key_part.shape[0]
    step_rows = 512

    def one_block(position, state):
        key_block = lax.dynamic_slice_in_dim(key_part, position * step_rows, step_rows, 0)
        value_block = lax.dynamic_slice_in_dim(value_part, position * step_rows, step_rows, 0)
        return attend_rows(state, key_block, value_block, position * step_rows)

    running = lax.fori_loop(0, row_count // step_rows, one_block, initial)
    top_score, denominator, numerator = running
    mixed = numerator / jnp.transpose(denominator)[:, :, None]
    return mixed.reshape(slab_len, local_width).astype(jnp.bfloat16)


def kernel(lat, w_hbm, slots_hbm, count_hbm, out, slots, count, local_sem, tokens, w, w_sem, kv, q, top, total, acc, send_sem, recv_sem, up_sem):
    z = lax.axis_index("frame")
    h = lax.axis_index("head")
    core = h % 2
    mate = h + 1 - 2 * core
    across = (h + 2) % 4
    rows, width_in = lat.shape
    width = w_hbm.shape[2]
    slab = 4 * rows
    heads = width // HD
    blocks = slots.shape[0]
    per_slab = slots.shape[2]
    block_rows = slab // blocks
    key_rows = slab // per_slab
    scale = HD ** (-0.5) * 1.4426950408889634

    w_copies = [
        pltpu.make_async_copy(w_hbm.at[j], w.at[:, pl.ds(place * width, width)], w_sem.at[place])
        for place, j in enumerate((1, 2, 0))
    ]
    for copy in w_copies:
        copy.start()

    half = z // 2
    end = z + half * (3 - 2 * z)
    firsts = [1 - end, 2, 3]
    others = [f + half * (3 - 2 * f) for f in firsts]

    barrier = pltpu.get_barrier_semaphore()

    def greet(frame, who):
        pl.semaphore_signal(barrier, inc=1, device_id={"frame": frame, "head": who}, device_id_type=MESH)

    greet(z, mate)
    greet(z, across)

    @pl.when(z > 0)
    def _():
        greet(z - 1, h)

    @pl.when(z < 3)
    def _():
        greet(z + 1, h)

    pl.semaphore_wait(barrier, jnp.where(end == 0, 3, 4))

    def copy_of(src, slot, number, frame, who):
        return pltpu.make_async_remote_copy(
            src_ref=src,
            dst_ref=tokens.at[slot],
            send_sem=send_sem.at[number],
            recv_sem=recv_sem.at[slot],
            device_id={"frame": frame, "head": who},
            device_id_type=MESH,
        )

    def lower_of(slot, number, frame, who):
        part = tokens.at[slot, pl.ds(0, rows // 2)]
        return pltpu.make_async_remote_copy(
            src_ref=part,
            dst_ref=part,
            send_sem=send_sem.at[number],
            recv_sem=recv_sem.at[slot],
            device_id={"frame": frame, "head": who},
            device_id_type=MESH,
        )

    def upper_of(b, number, frame):
        part = tokens.at[b * 4 + across, pl.ds(rows // 2, rows // 2)]
        return pltpu.make_async_remote_copy(
            src_ref=part,
            dst_ref=tokens.at[b * 4 + across, pl.ds(rows // 2, rows // 2)],
            send_sem=send_sem.at[number],
            recv_sem=up_sem.at[b // 3],
            device_id={"frame": frame, "head": h},
            device_id_type=MESH,
        )

    middle = end == 1
    outer = end == 0
    sends = []

    def send(src, slot, frame, who, when=None):
        copy = copy_of(src, slot, len(sends), frame, who)
        sends.append((copy, when))
        if when is None:
            copy.start()
        else:
            pl.when(when)(copy.start)

    def arrived(slot):
        copy_of(tokens.at[slot], slot, 0, z, mate).wait_recv()

    mine = z * 4 + h
    send(lat, mine, z, across)
    send(lat, mine, z - 1, h, z > 0)
    send(lat, mine, z + 1, h, z < 3)
    send(lat, mine, z, mate)
    local = [
        pltpu.make_async_copy(lat, tokens.at[mine], local_sem.at[0]),
        pltpu.make_async_copy(slots_hbm, slots, local_sem.at[1]),
        pltpu.make_async_copy(count_hbm, count, local_sem.at[2]),
    ]
    for copy in local:
        copy.start()

    def forward(number, when):
        b = others[number]
        slot = b * 4 + h
        sign = jnp.where(b > z, 1, -1)
        onward = z - sign
        goes = (onward >= 0) & (onward <= 3)
        base = 4 + 3 * number
        moves = [
            (copy_of(tokens.at[slot], slot, base, onward, h), goes),
            (copy_of(tokens.at[slot], slot, base + 2, z, mate), None),
        ]
        if number == 0:
            moves.append((copy_of(tokens.at[slot], slot, base + 1, z, across), outer))
            moves.append((lower_of(slot, base + 1, z, across), middle))
        elif number == 1:
            moves.append((copy_of(tokens.at[slot], slot, base + 1, z, across), None))
        else:
            moves.append((lower_of(slot, base + 1, z, across), None))

        def go():
            arrived(slot)
            for copy, wanted in moves[:1] + moves[2:] + moves[1:2]:
                if wanted is None:
                    copy.start()
                else:
                    pl.when(wanted)(copy.start)

        if when is None:
            go()
        else:
            pl.when(when)(go)
        return moves

    def complete(number, b):
        slot = b * 4 + across
        if number == 1:

            @pl.when(outer)
            def _():
                arrived(slot)

            @pl.when(middle)
            def _():
                lower_of(slot, 0, z, mate).wait_recv()

        elif number == 3:
            lower_of(slot, 0, z, mate).wait_recv()

            @pl.when(outer)
            def _():
                upper_of(b, 0, z + 1 - 2 * half).wait_recv()

        else:
            arrived(slot)
        copy = copy_of(tokens.at[slot], slot, 13 + number, z, mate)
        copy.start()
        return [(copy, None)]

    inward = z + 1 - 2 * half

    def pass_upper(b, number, frame):
        copy = upper_of(b, number, frame)

        @pl.when(middle)
        def _():
            copy.wait_recv()
            copy.start()

        return [(copy, middle)]

    def project(slot, rows_here, first, columns, store):
        x = tokens[pl.ds(slot, rows_here // rows)].reshape(rows_here, width_in)
        part = jnp.dot(x, w[:, pl.ds(first, columns)], preferred_element_type=jnp.float32)
        store[...] = part.astype(jnp.bfloat16)

    def whole(b):
        arrived(b * 4 + mate)
        arrived(b * 4 + (mate + 2) % 4)

    def attend(b, place, length, first, between=None):
        span = length * rows
        for tile in range(2 * width // 256):
            project(b * 4 + place, span, tile * 256, 256, kv.at[pl.ds(0, span), pl.ds(tile * 256, 256)])
        if between is not None:
            between()
        lane_block = (lax.broadcasted_iota(jnp.int32, (1, span), 1) + place * rows) // key_rows
        shades = []
        for a in range(blocks):
            listed = count[a, b]
            seen = jnp.zeros((1, span), jnp.float32)
            for s in range(per_slab):
                wanted = jnp.where(s < listed, slots[a, b, s], -1)
                seen = jnp.where(lane_block == wanted, 1.0, seen)
            shade = jnp.where(seen > 0.5, 0.0, masked_score)
            shades.append(jnp.broadcast_to(shade, (block_rows, span)))
        shade = jnp.concatenate(shades, axis=0)
        for n in range(heads):
            cols = pl.ds(n * HD, HD)
            scores = lax.dot_general(
                q[:, cols], kv[pl.ds(0, span), cols], (((1,), (1,)), ((), ())), preferred_element_type=jnp.float32
            )
            scores = scores * scale + shade
            peak = jnp.max(scores, axis=1, keepdims=True)
            if not first:
                peak = jnp.maximum(peak, top[n])
            shares = jnp.exp2(scores - peak)
            added = jnp.sum(shares, axis=1, keepdims=True)
            mixed = jnp.dot(
                shares.astype(jnp.bfloat16),
                kv[pl.ds(0, span), pl.ds(width + n * HD, HD)],
                preferred_element_type=jnp.float32,
            )
            if not first:
                keep = jnp.exp2(top[n] - peak)
                added = added + total[n] * keep
                mixed = mixed + acc[n] * keep
            top[n] = peak
            total[n] = added
            acc[n] = mixed

    late = []
    late += forward(0, None)
    late += forward(1, middle)
    late += complete(0, z)
    own_upper = upper_of(z, 17, inward)
    pl.when(outer)(own_upper.start)
    late.append((own_upper, outer))
    whole(z)
    for copy in local + w_copies:
        copy.wait()
    project(z * 4, slab, 2 * width, width, q)

    def pass_first():
        forward(1, outer)
        late.extend(forward(2, middle))
        late.extend(pass_upper(others[0], 18, inward))
        late.extend(complete(1, others[0]))

    def pass_second():
        forward(2, outer)
        late.extend(pass_upper(others[2], 19, z - 1 + 2 * half))
        late.extend(complete(2, others[1]))

    def pass_third():
        late.extend(complete(3, others[2]))

    attend(z, 0, 4, True, pass_first)
    whole(others[0])
    attend(others[0], 0, 4, False, pass_second)
    whole(others[1])
    attend(others[1], 0, 4, False, pass_third)
    whole(others[2])
    attend(others[2], 0, 4, False)
    for n in range(heads):
        out[:, pl.ds(n * HD, HD)] = (acc[n] / total[n]).astype(jnp.bfloat16)
    for copy, when in sends + late:
        if when is None:
            copy.wait_send()
        else:
            pl.when(when)(copy.wait_send)


def fused(latents, weights, key_slots, key_count):
    rows, width_in = latents.shape
    width = weights.shape[2]
    slab = 4 * rows
    heads = width // HD
    return pl.pallas_call(
        kernel,
        out_shape=jax.ShapeDtypeStruct((slab, width), jnp.bfloat16),
        in_specs=[
            pl.BlockSpec(memory_space=pltpu.HBM),
            pl.BlockSpec(memory_space=pltpu.HBM),
            pl.BlockSpec(memory_space=pltpu.HBM),
            pl.BlockSpec(memory_space=pltpu.HBM),
        ],
        out_specs=pl.BlockSpec(memory_space=pltpu.VMEM),
        scratch_shapes=[
            pltpu.SMEM(key_slots.shape, jnp.int32),
            pltpu.SMEM(key_count.shape, jnp.int32),
            pltpu.SemaphoreType.DMA((3,)),
            pltpu.VMEM((16, rows, width_in), jnp.bfloat16),
            pltpu.VMEM((width_in, 3 * width), jnp.bfloat16),
            pltpu.SemaphoreType.DMA((3,)),
            pltpu.VMEM((slab, 2 * width), jnp.bfloat16),
            pltpu.VMEM((slab, width), jnp.bfloat16),
            pltpu.VMEM((heads, slab, 1), jnp.float32),
            pltpu.VMEM((heads, slab, 1), jnp.float32),
            pltpu.VMEM((heads, slab, HD), jnp.float32),
            pltpu.SemaphoreType.DMA((20,)),
            pltpu.SemaphoreType.DMA((16,)),
            pltpu.SemaphoreType.DMA((2,)),
        ],
        compiler_params=pltpu.CompilerParams(
            collective_id=0, has_side_effects=True, vmem_limit_bytes=64 * 1024 * 1024
        ),
    )(latents, jnp.transpose(weights, (1, 0, 2)), key_slots, key_count)


def solution(mesh):
    small = mesh.shape["frame"] == 4 and mesh.shape["head"] == 4
    return jax.shard_map(
        fused if small else on_device,
        mesh=mesh,
        in_specs=(
            P(("video", "frame", "head"), None),
            P(None, None, "head"),
            P("frame", None, None),
            P("frame", None),
        ),
        out_specs=P(("video", "frame"), "head"),
        check_vma=False,
    )
```
